768 devices in a mesh: replica: 4 (over x_lo, core), shard: 192 (over x_hi, z, y).
Axes of the slice: x: 4 (x_hi: 2, x_lo: 2; x = x_hi * 2 + x_lo), y: 8, z: 12, core: 2. Of those that a mesh axis runs over, the one named last changes fastest.
Arguments:
- inner_params: bfloat16 [4, 15360, 4096], P('replica', 'shard'), may hold values from -6 to 6
- anchor: float32 [15360, 4096], P('shard'), may hold values from -6 to 6
- momentum: float32 [15360, 4096], P('shard'), may hold values from -2 to 2
- first_moment: bfloat16 [4, 15360, 4096], P('replica', 'shard'), may hold values from -0.59765625 to 0.59765625
- second_moment: bfloat16 [4, 15360, 4096], P('replica', 'shard'), may hold values from 0.0009994507 to 0.099609375
- activations: bfloat16 [4, 768, 4096], P('replica', 'shard'), may hold values from -6 to 6
- cotangent: bfloat16 [4, 15360, 768], P('replica', 'shard'), may hold values from -6 to 6
- spare_index: int32 [192], P('shard'), may hold values from 0 to 3
- peer_index: int32 [192], P('shard'), may hold values from 0 to 3
Outputs:
- anchor_new: float32 [15360, 4096], P('shard')
- momentum_new: float32 [15360, 4096], P('shard')
- update: float32 [4, 15360, 4096], P('replica', 'shard')
The draws below stay inside these ranges and needn't reach their ends.
Inputs may be any that keep to these rules, and one draw needn't show every extreme that they name: `spare_index`: a replica index for each block. `peer_index`: a replica index for each block; where it equals spare_index the spare keeps its own moments.
All inputs are finite; a program needn't handle non-finite values.
Results may differ from the reference program's by a relative error of at most 0.0018.
Values may be sent and summed in bfloat16 or wider, within the bound.
A program may use at most 64 MiB of HBM per device.

```python
import math
import jax
import jax.numpy as jnp
from jax import lax

D = 4096
FF = 15360
TOKENS = 768
N_REPLICA = 4
N_SHARD = 192


def with_ends(array, key, least, high):
    longest = array.shape.index(max(array.shape))
    spots = []
    for shift in (0, 1):
        where = [jax.random.randint(jax.random.fold_in(key, axis), (), 0, length) for axis, length in enumerate(array.shape)]
        where[longest] = (where[longest] + shift) % array.shape[longest]
        spots.append(tuple(where))
    return array.at[spots[0]].set(least).at[spots[1]].set(high)


def steps_of(stream_key, dims, shards, low, largest):
    level = 1.0
    for axis_at, parts in shards:
        steps = jax.random.uniform(jax.random.fold_in(jax.random.fold_in(stream_key, 6), axis_at), (parts,), jnp.float32, low / len(shards), largest / len(shards))
        level = level * jnp.repeat(jnp.exp(steps), dims[axis_at] // parts).reshape((-1,) + (1,) * (len(dims) - 1 - axis_at))
    return level


def noise(own_key, dims, deviation, limit, pieces=(), kind=jnp.bfloat16):
    loudness = steps_of(own_key, dims, pieces, -0.22, 0.18) if pieces else 1.0
    values = jax.random.normal(own_key, dims, jnp.float32) * deviation * loudness
    return jnp.minimum(jnp.maximum(values, -limit), limit).astype(kind)


def setup_inputs(seed: int = 0) -> dict:
    key_of = jax.random.split(jax.random.key(seed), 10)
    return {
        "inner_params": noise(key_of[0], (N_REPLICA, FF, D), 1.0, 6.0, ((0, 4), (1, 192))),
        "anchor": noise(key_of[1], (FF, D), 1.0, 6.0, ((0, 192),), jnp.float32),
        "momentum": noise(key_of[2], (FF, D), 0.3, 2.0, ((0, 192),), jnp.float32),
        "first_moment": noise(key_of[3], (N_REPLICA, FF, D), 0.1, 0.59765625, ((0, 4), (1, 192))),
        "second_moment": jnp.clip(jnp.exp(math.log(0.099609375) - 4.6018058 * jax.random.uniform(key_of[4], (N_REPLICA, FF, D), jnp.float32) ** steps_of(key_of[4], (N_REPLICA, FF, D), ((0, 4), (1, 192)), -0.2, 0.2)), 0.0009994507, 0.099609375).astype(jnp.bfloat16),
        "activations": noise(key_of[5], (N_REPLICA, TOKENS, D), 1.0, 6.0, ((0, 4), (1, 192))),
        "cotangent": noise(key_of[6], (N_REPLICA, FF, TOKENS), 1.0, 6.0, ((0, 4), (1, 192))),
        "spare_index": with_ends(jax.random.randint(key_of[7], (N_SHARD,), 0, N_REPLICA), jax.random.fold_in(key_of[7], 1), 0, N_REPLICA - 1).astype(jnp.int32),
        "peer_index": with_ends(jax.random.randint(key_of[8], (N_SHARD,), 0, N_REPLICA), jax.random.fold_in(key_of[8], 1), 0, N_REPLICA - 1).astype(jnp.int32),
    }


outer_rate = 0.7
nesterov_mu = 0.9
beta_one = 0.9
beta_two = 0.95
bias_one = 1.0 - 0.9 ** 40
bias_two = 1.0 - 0.95 ** 40
adam_eps = 1e-08
decay_rate = 0.1

def slope(pre):
    sigma = jax.nn.sigmoid(pre)
    return sigma * (1.0 + pre * (1.0 - sigma))

def reference(inner_params, anchor, momentum, first_moment, second_moment, activations, cotangent, spare_index, peer_index):
    block_rows = FF // N_SHARD
    spare_rows = jnp.repeat(spare_index, block_rows)[:, None]
    peer_rows = jnp.repeat(peer_index, block_rows)[:, None]
    summed = jnp.zeros(anchor.shape, jnp.float32)
    for replica in range(N_REPLICA):
        healthy = (spare_rows != replica).astype(jnp.float32)
        summed = summed + (anchor - inner_params[replica].astype(jnp.float32)) * healthy
    average = summed / (N_REPLICA - 1)
    momentum_new = nesterov_mu * momentum + average
    anchor_new = anchor - outer_rate * (average + nesterov_mu * momentum_new)
    weights = anchor_new.astype(jnp.bfloat16)
    root = math.sqrt(D)

    def replica_update(replica):
        source = jnp.where(replica == spare_rows, peer_rows, replica).astype(jnp.int32)
        first_used = jnp.zeros(anchor.shape, jnp.float32)
        second_used = jnp.zeros(anchor.shape, jnp.float32)
        for other in range(N_REPLICA):
            picked = source == other
            first_used = jnp.where(picked, first_moment[other].astype(jnp.float32), first_used)
            second_used = jnp.where(picked, second_moment[other].astype(jnp.float32), second_used)
        tokens_here = lax.dynamic_index_in_dim(activations, replica, 0, keepdims=False)
        cot_here = lax.dynamic_index_in_dim(cotangent, replica, 0, keepdims=False)
        pre = lax.dot_general(weights, tokens_here, (((1,), (1,)), ((), ())), preferred_element_type=jnp.float32) / root
        grad_pre = (cot_here.astype(jnp.float32) * slope(pre)).astype(jnp.bfloat16)
        gradient = jnp.dot(grad_pre, tokens_here, preferred_element_type=jnp.float32) / root
        first = beta_one * first_used + (1.0 - beta_one) * gradient
        second = beta_two * second_used + (1.0 - beta_two) * gradient * gradient
        return first / bias_one / (jnp.sqrt(second / bias_two) + adam_eps) + decay_rate * anchor_new
    update = lax.map(replica_update, jnp.arange(N_REPLICA, dtype=jnp.int32))
    return (anchor_new, momentum_new, update)
```

```python
import functools

import jax
import jax.numpy as jnp
import numpy as np
from jax import lax
from jax.experimental import pallas as pl
from jax.experimental.pallas import tpu as pltpu
from jax.sharding import PartitionSpec as P

outer_rate = 0.7
nesterov_mu = 0.9
beta_one = 0.9
beta_two = 0.95
bias_one = 1.0 - 0.9**40
bias_two = 1.0 - 0.95**40
adam_eps = 1e-08
decay_rate = 0.1

NY, NZ = 8, 12
ROWS, D, TOK = 80, 4096, 768
HALF = D // 2
BR, BC = 16, 1024
PIECES = 4
ZP, YP = NZ // PIECES, NY // PIECES
f32, bf16 = jnp.float32, jnp.bfloat16


def slot(hops, way, ring):
    if hops == 0:
        return 0
    if 2 * hops == ring:
        return ring - 1
    return 2 * hops - 1 if way > 0 else 2 * hops


def offset_of(place, ring):
    if place == 0:
        return 0
    if place == ring - 1:
        return ring // 2
    hops = (place + 1) // 2
    return (ring - hops) if place % 2 else hops


GROUPS = [
    ("a", 0, 1, 0), ("a", 1, 1, 48), ("a", 2, 1, 96), ("b", 0, 1, 144), ("b", 1, 2, 176),
    ("a", 3, 1, 256), ("a", 4, 1, 304), ("b", 3, 2, 352), ("b", 5, 2, 416),
    ("a", 5, 1, 512), ("a", 6, 1, 560), ("b", 7, 2, 608),
    ("a", 7, 1, 768), ("b", 9, 2, 816), ("b", 11, 1, 880),
]
PADS = [(240, 256), (480, 512), (672, 768), (912, 1024)]


def token_table():
    table = np.zeros((8, 1024), np.int32)
    table[4] = 1
    for which, first, count, base in GROUPS:
        for row in range(first, first + count):
            for col in range(NZ if which == "a" else NY):
                yi, zi = (row, col) if which == "a" else (col, row)
                for t in range(4):
                    table[0, base] = offset_of(yi, NY)
                    table[1, base] = offset_of(zi, NZ)
                    table[2, base] = 0 if which == "a" else 1
                    table[3, base] = t
                    table[4, base] = 0
                    base += 1
    return table


def kernel(
    inner_ref, anchor_ref, momentum_ref, first_ref, second_ref, act_ref, cot_ref, spare_ref, peer_ref, table_ref,
    anchor_out, momentum_out, update_out,
    ga, gb, x, act_v, act_f, pb, an, mo, w, fm, mh, sel, rx, ca, cb, acc, cot, cotp, gp, perm, upd,
    load_sem, a1_s, a1_r, a2_s, a2_r, b1_s, b1_r, b2_s, b2_r, x_s, x_r, p_s, p_r, m_s, m_r, out_sem,
):
    r = lax.axis_index("replica")
    s = lax.axis_index("shard")
    core = r % 2
    xlo = r // 2
    y = s % NY
    z = (s // NY) % NZ
    xh = s // (NY * NZ)
    mate = r + 1 - 2 * core
    across = (r + 2) % 4
    far_mate = mate + 2 - 4 * xlo

    def at(rep, sh):
        return {"replica": rep, "shard": sh}

    y_to = {1: at(r, s - y + (y + 1) % NY), -1: at(r, s - y + (y + NY - 1) % NY)}
    z_to = {
        1: at(r, (xh * NZ + (z + 1) % NZ) * NY + y),
        -1: at(r, (xh * NZ + (z + NZ - 1) % NZ) * NY + y),
    }
    plane_to = at(r, (s + NY * NZ) % (2 * NY * NZ))
    mate_to = at(mate, s)
    across_to = at(across, s)

    loads = {}

    def load(name, i, src, dst):
        loads[name] = pltpu.make_async_copy(src, dst, load_sem.at[i])
        loads[name].start()

    load("act", 0, act_ref, act_v)
    load("inner", 1, inner_ref, pb.at[0])
    load("anchor", 2, anchor_ref, an)
    load("momentum", 3, momentum_ref, mo)
    load("first", 4, first_ref, fm.at[0])
    load("second", 5, second_ref, fm.at[1])
    load("cot", 6, cot_ref, cot)

    barrier = pltpu.get_barrier_semaphore()
    for to in (y_to[1], y_to[-1], z_to[1], z_to[-1], plane_to, mate_to, across_to):
        pl.semaphore_signal(barrier, inc=1, device_id=to, device_id_type=pl.DeviceIdType.MESH)

    loads["act"].wait()
    for q in range(4):
        act_f[4 * q : 4 * q + 4, :] = act_v[:, q * BC : (q + 1) * BC].astype(f32)
    ga[0:BR, :] = act_f[...].astype(bf16)

    pl.semaphore_wait(barrier, 7)

    made = {}

    def copy(key, src, dst, ss, rs, to):
        made[key] = pltpu.make_async_remote_copy(
            src_ref=src, dst_ref=dst, send_sem=ss, recv_sem=rs, device_id=to, device_id_type=pl.DeviceIdType.MESH
        )

    def ga_at(yi, zi, n):
        return ga.at[pl.ds((yi * NZ + zi) * BR, n * BR), :]

    def gb_at(zi, yi, n):
        return gb.at[pl.ds((zi * NY + yi) * BR, n * BR), :]

    def has(hops, way, ring, piece=None):
        if 2 * hops < ring:
            return True
        if 2 * hops > ring:
            return False
        if piece is None:
            return way > 0
        return (way > 0) == (piece < PIECES // 2)

    for way in (1, -1):
        for k in range(1, NZ // 2 + 1):
            a, b = slot(k - 1, way, NZ), slot(k, way, NZ)
            if has(k, way, NZ):
                copy(("a1", way, k), ga_at(0, a, 1), ga_at(0, b, 1), a1_s.at[b], a1_r.at[b], z_to[way])
            for q in range(PIECES):
                if has(k, way, NZ, q):
                    copy(("b2", way, k, q), gb_at(a, q * YP, YP), gb_at(b, q * YP, YP), b2_s.at[b, q], b2_r.at[b, q], z_to[way])
        for k in range(1, NY // 2 + 1):
            a, b = slot(k - 1, way, NY), slot(k, way, NY)
            if has(k, way, NY):
                copy(("b1", way, k), gb_at(0, a, 1), gb_at(0, b, 1), b1_s.at[b], b1_r.at[b], y_to[way])
            for q in range(PIECES):
                if has(k, way, NY, q):
                    copy(("a2", way, k, q), ga_at(a, q * ZP, ZP), ga_at(b, q * ZP, ZP), a2_s.at[b, q], a2_r.at[b, q], y_to[way])
    copy(("x",), ga_at(0, 0, 1), gb_at(0, 0, 1), x_s, x_r, plane_to)
    for j in range(5):
        rows = pl.ds(16 * j, 16)
        copy(("px", j), inner_ref.at[rows, :], pb.at[2, rows, :], p_s.at[0, j], p_r.at[0, j], across_to)
        copy(("pm", j), inner_ref.at[rows, :], pb.at[1, rows, :], p_s.at[1, j], p_r.at[1, j], mate_to)
        copy(("pf", j), pb.at[2, rows, :], pb.at[3, rows, :], p_s.at[2, j], p_r.at[2, j], mate_to)
    theirs = pl.ds(pl.multiple_of((1 - core) * HALF, HALF), HALF)
    for i, ref in enumerate((first_ref, second_ref)):
        copy(("mh", i), ref.at[:, theirs], mh.at[i], m_s.at[0, i], m_r.at[0, i], mate_to)
        copy(("mx", i), sel.at[i], rx.at[i], m_s.at[1, i], m_r.at[1, i], across_to)
        copy(("mc", i), ca.at[i], cb.at[i], m_s.at[2, i], m_r.at[2, i], mate_to)

    started, received = [], set()

    def start(*key):
        if key in made:
            made[key].start()
            assert key not in started
            started.append(key)

    def take(*key):
        if key in made:
            assert key in started and key not in received
            made[key].wait_recv()
            received.add(key)

    events = []

    def event(time, what):
        events.append((time, len(events), what))

    spare = spare_ref[0]
    peer = peer_ref[0]
    not_spare = [(spare != who).astype(f32) for who in (r, mate, across, far_mate)]

    def a1(k):
        for way in (1, -1):
            take("a1", way, k)
            start("a1", way, k + 1)

    def b1(k):
        for way in (1, -1):
            take("b1", way, k)
            start("b1", way, k + 1)

    def step(name, k, q):
        for way in (1, -1):
            if k:
                take(name, way, k, q)
            start(name, way, k + 1, q)

    def plane():
        take("x")
        start("b1", 1, 1)
        start("b1", -1, 1)

    a_in = {1: [0], 3: [1], 4: [2], 6: [3]}
    b_in = {1: [0], 2: [1], 3: [2], 4: [3]}
    for k in range(1, NZ // 2 + 1):
        event(2.2 * k, functools.partial(a1, k))
    event(2.9, plane)
    for k in range(1, NY // 2 + 1):
        event(2.9 + 2.2 * k, functools.partial(b1, k))
    for k, pieces in a_in.items():
        for q in pieces:
            event(2.2 * k + (0.8 if k == 1 else 0.01), functools.partial(step, "a2", 0, q))
    for k, pieces in b_in.items():
        for q in pieces:
            event(2.9 + 2.2 * k + 0.01, functools.partial(step, "b2", 0, q))

    def a2_time(k, q):
        return 6 + 12 * (k - 1) + 3 * ((q % 2 if 2 * k == NY else q) + 1) + 2

    def b2_time(k, q):
        return 10 + 8 * (k - 1) + 2 * ((q % 2 if 2 * k == NZ else q) + 1) + 2

    for q in range(PIECES):
        for k in range(1, NY // 2 + 1):
            event(a2_time(k, q), functools.partial(step, "a2", k, q))
        for k in range(1, NZ // 2 + 1):
            event(b2_time(k, q), functools.partial(step, "b2", k, q))

    def pass_on(j):
        take("px", j)
        start("pf", j)

    def outer(j):
        if j == 0:
            for name in ("inner", "anchor", "momentum"):
                loads[name].wait()
        take("pm", j)
        take("pf", j)
        rows = slice(16 * j, 16 * j + 16)

        @pl.loop(0, D // 512)
        def _(i):
            cols = pl.ds(pl.multiple_of(i * 512, 512), 512)
            a = an[rows, cols]
            total = jnp.zeros_like(a)
            for n in range(4):
                total = total + (a - pb[n, rows, cols].astype(f32)) * not_spare[n]
            average = total / 3.0
            fresh = nesterov_mu * mo[rows, cols] + average
            mo[rows, cols] = fresh
            a = a - outer_rate * (average + nesterov_mu * fresh)
            an[rows, cols] = a
            w[rows, cols] = a.astype(bf16)

    outs = {}

    def ship(name, i, src, dst):
        outs[name] = pltpu.make_async_copy(src, dst, out_sem.at[i])
        outs[name].start()

    for j in range(5):
        event(4 * (j + 1) + 2.5, functools.partial(pass_on, j))
        event(4 * (j + 1) + 5.5, functools.partial(outer, j))

    def ship_outer():
        ship("anchor", 0, an, anchor_out)
        ship("momentum", 1, mo, momentum_out)

    event(25.6, ship_outer)

    def choose():
        for name in ("first", "second"):
            loads[name].wait()
        for i in range(2):
            take("mh", i)

            @pl.loop(0, HALF // 512)
            def _(n):
                cols = pl.ds(pl.multiple_of(n * 512, 512), 512)
                high = pl.ds(pl.multiple_of(n * 512 + HALF, 512), 512)
                mine = jnp.where(core == 0, fm[i, :, cols].astype(f32), fm[i, :, high].astype(f32))
                sel[i, :, cols] = jnp.where(peer == mate, mh[i, :, cols].astype(f32), mine).astype(bf16)

            start("mx", i)

    def settle(i):
        take("mx", i)

        @pl.loop(0, HALF // 512)
        def _(n):
            cols = pl.ds(pl.multiple_of(n * 512, 512), 512)
            here = jnp.logical_or(peer == r, peer == mate)
            ca[i, :, cols] = jnp.where(here, sel[i, :, cols].astype(f32), rx[i, :, cols].astype(f32)).astype(bf16)

        start("mc", i)

    def adopt(i):
        take("mc", i)

        @pl.loop(0, HALF // 512)
        def _(n):
            for half in range(2):
                cols = pl.ds(pl.multiple_of(n * 512, 512), 512)
                dest = pl.ds(pl.multiple_of(n * 512 + half * HALF, 512), 512)
                new = jnp.where(core == half, ca[i, :, cols].astype(f32), cb[i, :, cols].astype(f32))
                fm[i, :, dest] = jnp.where(spare == r, new, fm[i, :, dest].astype(f32)).astype(bf16)

    event(4.0, choose)
    for i in range(2):
        event(34.2 + 10 * i, functools.partial(settle, i))
        event(37.2 + 10 * i, functools.partial(adopt, i))

    def prepare():
        for lo, hi in PADS:
            x[lo:hi, :] = jnp.zeros((hi - lo, D), bf16)
        for nth, blocks in enumerate((12, 16, 8)):
            n = blocks * BR
            out = lax.broadcasted_iota(jnp.int32, (n, n), 0)
            src = lax.broadcasted_iota(jnp.int32, (n, n), 1)
            quarter = (src % BR) // 4
            goal = quarter * (blocks * 4) + (src // BR) * 4 + src % 4
            perm[nth, 0:n, 0:n] = jnp.where(out == goal, 1.0, 0.0).astype(bf16)

    def reorder_cot(c):
        if c == 0:
            loads["cot"].wait()
        cols = slice(256 * c, 256 * c + 256)
        dy, dz, other, t, void = (table_ref[i : i + 1, cols] for i in range(5))
        yy = dy + y
        yy = jnp.where(yy >= NY, yy - NY, yy)
        zz = dz + z
        zz = jnp.where(zz >= NZ, zz - NZ, zz)
        hh = jnp.where(other == 1, 1 - xh, xh)
        token = ((hh * NZ + zz) * NY + yy) * 4 + t
        token = jnp.where(void == 1, -1, token)
        pick = lax.broadcasted_iota(jnp.int32, (TOK, 256), 0) == token
        cotp[:, cols] = jnp.dot(cot[...], jnp.where(pick, 1.0, 0.0).astype(bf16), preferred_element_type=f32)

    def arrange(which, first, count, base):
        buf, per = (ga, NZ) if which == "a" else (gb, NY)
        blocks = per * count
        n = blocks * BR
        nth = {12: 0, 16: 1, 8: 2}[blocks]

        for i in range(BC // 256):
            cols = slice(i * 256, i * 256 + 256)
            got = jnp.dot(
                perm[nth, 0:n, 0:n], buf[first * per * BR : first * per * BR + n, cols], preferred_element_type=f32
            ).astype(bf16)
            for q in range(4):
                x[base : base + blocks * 4, q * BC + i * 256 : q * BC + i * 256 + 256] = got[
                    q * blocks * 4 : (q + 1) * blocks * 4
                ]

    def slopes(c):
        rows = slice(256 * c, 256 * c + 256)
        pre = lax.dot_general(w[...], x[rows, :], (((1,), (1,)), ((), ())), preferred_element_type=f32) / 64.0
        sigma = jax.nn.sigmoid(pre)
        gp[...] = (cotp[:, rows] * (sigma * (1.0 + pre * (1.0 - sigma)))).astype(bf16)

    def gradient(c):
        rows = slice(256 * c, 256 * c + 256)
        slopes(c)

        @pl.loop(0, D // 512)
        def _(i):
            cols = pl.ds(pl.multiple_of(i * 512, 512), 512)
            part = jnp.dot(gp[...], x[rows, cols], preferred_element_type=f32)
            if c == 0:
                acc[:, cols] = part
            else:
                acc[:, cols] += part

    event(0.5, prepare)
    for c in range(4):
        event(1.0 + 1.1 * c + (0.15 if c else 0), functools.partial(reorder_cot, c))
    for which, first, count, base in GROUPS:
        last = first + count - 1
        if last == 0:
            ready = 2.2 * 6 + 0.1 if which == "a" else 2.9 + 2.2 * 4 + 0.1
        else:
            hops = (last + 1) // 2
            ready = (a2_time if which == "a" else b2_time)(hops, 3) + 0.1
        event(ready, functools.partial(arrange, which, first, count, base))
    event(27.0, functools.partial(gradient, 0))
    event(38.3, functools.partial(gradient, 1))
    event(46.3, functools.partial(gradient, 2))

    for way in (1, -1):
        start("a1", way, 1)
    start("x")
    for j in range(5):
        start("px", j)
    for i in range(2):
        start("mh", i)
    for j in range(5):
        start("pm", j)
    sent = 0
    for time, _, what in sorted(events, key=lambda e: e[:2]):
        what()

    c = 3
    rows = slice(256 * c, 256 * c + 256)
    slopes(c)

    @pl.loop(0, D // 256)
    def _(i):
        cols = pl.ds(pl.multiple_of(i * 256, 256), 256)
        g = (acc[:, cols] + jnp.dot(gp[...], x[rows, cols], preferred_element_type=f32)) * (1.0 / 64.0)
        first = beta_one * fm[0, :, cols].astype(f32) + (1.0 - beta_one) * g
        second = beta_two * fm[1, :, cols].astype(f32) + (1.0 - beta_two) * g * g
        upd[:, cols] = first / bias_one / (jnp.sqrt(second / bias_two) + adam_eps) + decay_rate * an[:, cols]

    ship("update", 2, upd, update_out)
    assert received == set(made) and len(started) == len(made)
    for key in started:
        made[key].wait_send()
    for name in outs:
        outs[name].wait()


def local(inner_params, anchor, momentum, first_moment, second_moment, activations, cotangent, spare_index, peer_index):
    hbm = pl.BlockSpec(memory_space=pltpu.MemorySpace.HBM)
    smem = pl.BlockSpec(memory_space=pltpu.SMEM)
    vmem = pl.BlockSpec(memory_space=pltpu.VMEM)
    dma = pltpu.SemaphoreType.DMA
    whole = jax.ShapeDtypeStruct((ROWS, D), f32)
    anchor_new, momentum_new, update = pl.pallas_call(
        kernel,
        out_shape=(whole, whole, whole),
        in_specs=[hbm] * 7 + [smem] * 2 + [vmem],
        out_specs=(hbm, hbm, hbm),
        scratch_shapes=[
            pltpu.VMEM((NY * NZ * BR, BC), bf16),
            pltpu.VMEM((NY * NZ * BR, BC), bf16),
            pltpu.VMEM((1024, D), bf16),
            pltpu.VMEM((4, D), bf16),
            pltpu.VMEM((BR, BC), f32),
            pltpu.VMEM((4, ROWS, D), bf16),
            pltpu.VMEM((ROWS, D), f32),
            pltpu.VMEM((ROWS, D), f32),
            pltpu.VMEM((ROWS, D), bf16),
            pltpu.VMEM((2, ROWS, D), bf16),
            pltpu.VMEM((2, ROWS, HALF), bf16),
            pltpu.VMEM((2, ROWS, HALF), bf16),
            pltpu.VMEM((2, ROWS, HALF), bf16),
            pltpu.VMEM((2, ROWS, HALF), bf16),
            pltpu.VMEM((2, ROWS, HALF), bf16),
            pltpu.VMEM((ROWS, D), f32),
            pltpu.VMEM((ROWS, TOK), bf16),
            pltpu.VMEM((ROWS, 1024), f32),
            pltpu.VMEM((ROWS, 256), bf16),
            pltpu.VMEM((3, 256, 256), bf16),
            pltpu.VMEM((ROWS, D), f32),
            dma((7,)),
            dma((NZ,)), dma((NZ,)),
            dma((NY, PIECES)), dma((NY, PIECES)),
            dma((NY,)), dma((NY,)),
            dma((NZ, PIECES)), dma((NZ, PIECES)),
            dma, dma,
            dma((3, 5)), dma((3, 5)),
            dma((3, 2)), dma((3, 2)),
            dma((3,)),
        ],
        compiler_params=pltpu.CompilerParams(
            collective_id=0, has_side_effects=True, vmem_limit_bytes=52 * 1024 * 1024
        ),
        cost_estimate=pl.CostEstimate(flops=2 * 2 * ROWS * D * TOK, bytes_accessed=9 << 20, transcendentals=ROWS * TOK),
    )(
        inner_params[0], anchor, momentum, first_moment[0], second_moment[0], activations[0], cotangent[0],
        spare_index, peer_index, jnp.asarray(token_table()),
    )
    return anchor_new, momentum_new, update[None]


def solution(mesh):
    placed = (
        P("replica", "shard", None),
        P("shard", None),
        P("shard", None),
        P("replica", "shard", None),
        P("replica", "shard", None),
        P("replica", "shard", None),
        P("replica", "shard", None),
        P("shard"),
        P("shard"),
    )
    return jax.shard_map(
        local,
        mesh=mesh,
        in_specs=placed,
        out_specs=(P("shard", None), P("shard", None), P("replica", "shard", None)),
        check_vma=False,
    )
```

```python
import functools

import jax
import jax.numpy as jnp
import numpy as np
from jax import lax
from jax.experimental import pallas as pl
from jax.experimental.pallas import tpu as pltpu
from jax.sharding import PartitionSpec as P

outer_rate = 0.7
nesterov_mu = 0.9
beta_one = 0.9
beta_two = 0.95
bias_one = 1.0 - 0.9**40
bias_two = 1.0 - 0.95**40
adam_eps = 1e-08
decay_rate = 0.1

NY, NZ = 8, 12
ROWS, D, TOK = 80, 4096, 768
HALF = D // 2
BR, BC = 16, 1024
PIECES = 4
ZP, YP = NZ // PIECES, NY // PIECES
f32, bf16 = jnp.float32, jnp.bfloat16


def slot(hops, way, ring):
    if hops == 0:
        return 0
    if 2 * hops == ring:
        return ring - 1
    return 2 * hops - 1 if way > 0 else 2 * hops


def offset_of(place, ring):
    if place == 0:
        return 0
    if place == ring - 1:
        return ring // 2
    hops = (place + 1) // 2
    return (ring - hops) if place % 2 else hops


GROUPS = [
    ("a", 0, 1, 0), ("a", 1, 1, 48), ("a", 2, 1, 96), ("b", 0, 1, 144), ("b", 1, 2, 176),
    ("a", 3, 1, 256), ("a", 4, 1, 304), ("b", 3, 2, 352), ("b", 5, 2, 416),
    ("a", 5, 1, 512), ("a", 6, 1, 560), ("b", 7, 2, 608),
    ("a", 7, 1, 768), ("b", 9, 2, 816), ("b", 11, 1, 880),
]
PADS = [(240, 256), (480, 512), (672, 768), (912, 1024)]


def token_table():
    table = np.zeros((8, 1024), np.int32)
    table[4] = 1
    for which, first, count, base in GROUPS:
        for row in range(first, first + count):
            for col in range(NZ if which == "a" else NY):
                yi, zi = (row, col) if which == "a" else (col, row)
                for t in range(4):
                    table[0, base] = offset_of(yi, NY)
                    table[1, base] = offset_of(zi, NZ)
                    table[2, base] = 0 if which == "a" else 1
                    table[3, base] = t
                    table[4, base] = 0
                    base += 1
    return table


def kernel(
    inner_ref, anchor_ref, momentum_ref, first_ref, second_ref, act_ref, cot_ref, spare_in, peer_in, table_in,
    average_out, first_out, second_out, gradient_out,
    ga, gb, x, act_v, act_f, pb, an, mo, w, fm, mh, sel, rx, ca, cb, acc, cot, cotp, gp, perm, table_ref, spare_ref, peer_ref,
    load_sem, a1_s, a1_r, a2_s, a2_r, b1_s, b1_r, b2_s, b2_r, x_s, x_r, p_s, p_r, m_s, m_r, out_sem,
):
    r = lax.axis_index("replica")
    s = lax.axis_index("shard")
    core = r % 2
    xlo = r // 2
    y = s % NY
    z = (s // NY) % NZ
    xh = s // (NY * NZ)
    mate = r + 1 - 2 * core
    across = (r + 2) % 4
    far_mate = mate + 2 - 4 * xlo

    def at(rep, sh):
        return {"replica": rep, "shard": sh}

    y_to = {1: at(r, s - y + (y + 1) % NY), -1: at(r, s - y + (y + NY - 1) % NY)}
    z_to = {
        1: at(r, (xh * NZ + (z + 1) % NZ) * NY + y),
        -1: at(r, (xh * NZ + (z + NZ - 1) % NZ) * NY + y),
    }
    plane_to = at(r, (s + NY * NZ) % (2 * NY * NZ))
    mate_to = at(mate, s)
    across_to = at(across, s)

    loads = {}

    def load(name, i, src, dst):
        loads[name] = pltpu.make_async_copy(src, dst, load_sem.at[i])
        loads[name].start()

    load("act", 0, act_ref, act_v)
    load("inner", 1, inner_ref, pb.at[0])
    load("anchor", 2, anchor_ref, an)
    load("momentum", 3, momentum_ref, mo)
    load("first", 4, first_ref, fm.at[0])
    load("second", 5, second_ref, fm.at[1])
    load("cot", 6, cot_ref, cot)
    load("table", 7, table_in, table_ref)
    load("spare", 8, spare_in, spare_ref)
    load("peer", 9, peer_in, peer_ref)

    barrier = pltpu.get_barrier_semaphore()
    for to in (y_to[1], y_to[-1], z_to[1], z_to[-1], plane_to, mate_to, across_to):
        pl.semaphore_signal(barrier, inc=1, device_id=to, device_id_type=pl.DeviceIdType.MESH)

    loads["act"].wait()
    for q in range(4):
        act_f[4 * q : 4 * q + 4, :] = act_v[:, q * BC : (q + 1) * BC].astype(f32)
    ga[0:BR, :] = act_f[...].astype(bf16)

    pl.semaphore_wait(barrier, 7)

    made = {}

    def copy(key, src, dst, ss, rs, to):
        made[key] = pltpu.make_async_remote_copy(
            src_ref=src, dst_ref=dst, send_sem=ss, recv_sem=rs, device_id=to, device_id_type=pl.DeviceIdType.MESH
        )

    def ga_at(yi, zi, n):
        return ga.at[pl.ds((yi * NZ + zi) * BR, n * BR), :]

    def gb_at(zi, yi, n):
        return gb.at[pl.ds((zi * NY + yi) * BR, n * BR), :]

    def has(hops, way, ring, piece=None):
        if 2 * hops < ring:
            return True
        if 2 * hops > ring:
            return False
        if piece is None:
            return way > 0
        return (way > 0) == (piece < PIECES // 2)

    for way in (1, -1):
        for k in range(1, NZ // 2 + 1):
            a, b = slot(k - 1, way, NZ), slot(k, way, NZ)
            if has(k, way, NZ):
                copy(("a1", way, k), ga_at(0, a, 1), ga_at(0, b, 1), a1_s.at[b], a1_r.at[b], z_to[way])
            for q in range(PIECES):
                if has(k, way, NZ, q):
                    copy(("b2", way, k, q), gb_at(a, q * YP, YP), gb_at(b, q * YP, YP), b2_s.at[b, q], b2_r.at[b, q], z_to[way])
        for k in range(1, NY // 2 + 1):
            a, b = slot(k - 1, way, NY), slot(k, way, NY)
            if has(k, way, NY):
                copy(("b1", way, k), gb_at(0, a, 1), gb_at(0, b, 1), b1_s.at[b], b1_r.at[b], y_to[way])
            for q in range(PIECES):
                if has(k, way, NY, q):
                    copy(("a2", way, k, q), ga_at(a, q * ZP, ZP), ga_at(b, q * ZP, ZP), a2_s.at[b, q], a2_r.at[b, q], y_to[way])
    copy(("x",), ga_at(0, 0, 1), gb_at(0, 0, 1), x_s, x_r, plane_to)
    for j in range(5):
        rows = pl.ds(16 * j, 16)
        copy(("px", j), inner_ref.at[rows, :], pb.at[2, rows, :], p_s.at[0, j], p_r.at[0, j], across_to)
        copy(("pm", j), inner_ref.at[rows, :], pb.at[1, rows, :], p_s.at[1, j], p_r.at[1, j], mate_to)
        copy(("pf", j), pb.at[2, rows, :], pb.at[3, rows, :], p_s.at[2, j], p_r.at[2, j], mate_to)
    theirs = pl.ds(pl.multiple_of((1 - core) * HALF, HALF), HALF)
    for i, ref in enumerate((first_ref, second_ref)):
        copy(("mh", i), ref.at[:, theirs], mh.at[i], m_s.at[0, i], m_r.at[0, i], mate_to)
        copy(("mx", i), sel.at[i], rx.at[i], m_s.at[1, i], m_r.at[1, i], across_to)
        copy(("mc", i), ca.at[i], cb.at[i], m_s.at[2, i], m_r.at[2, i], mate_to)

    started, received = [], set()

    def start(*key):
        if key in made:
            made[key].start()
            assert key not in started
            started.append(key)

    def take(*key):
        if key in made:
            assert key in started and key not in received
            made[key].wait_recv()
            received.add(key)

    events = []

    def event(time, what):
        events.append((time, len(events), what))

    loads["spare"].wait()
    loads["peer"].wait()
    spare = spare_ref[0]
    peer = peer_ref[0]
    not_spare = [(spare != who).astype(f32) for who in (r, mate, across, far_mate)]

    def a1(k):
        for way in (1, -1):
            take("a1", way, k)
            start("a1", way, k + 1)

    def b1(k):
        for way in (1, -1):
            take("b1", way, k)
            start("b1", way, k + 1)

    def step(name, k, q):
        for way in (1, -1):
            if k:
                take(name, way, k, q)
            start(name, way, k + 1, q)

    def plane():
        take("x")
        start("b1", 1, 1)
        start("b1", -1, 1)

    a_in = {1: [0], 3: [1], 4: [2], 6: [3]}
    b_in = {1: [0], 2: [1], 3: [2], 4: [3]}
    for k in range(1, NZ // 2 + 1):
        event(2.2 * k, functools.partial(a1, k))
    event(2.9, plane)
    for k in range(1, NY // 2 + 1):
        event(2.9 + 2.2 * k, functools.partial(b1, k))
    for k, pieces in a_in.items():
        for q in pieces:
            event(2.2 * k + (0.8 if k == 1 else 0.01), functools.partial(step, "a2", 0, q))
    for k, pieces in b_in.items():
        for q in pieces:
            event(2.9 + 2.2 * k + 0.01, functools.partial(step, "b2", 0, q))

    def a2_time(k, q):
        return 6 + 12 * (k - 1) + 3 * ((q % 2 if 2 * k == NY else q) + 1) + 2

    def b2_time(k, q):
        return 10 + 8 * (k - 1) + 2 * ((q % 2 if 2 * k == NZ else q) + 1) + 2

    for q in range(PIECES):
        for k in range(1, NY // 2 + 1):
            event(a2_time(k, q), functools.partial(step, "a2", k, q))
        for k in range(1, NZ // 2 + 1):
            event(b2_time(k, q), functools.partial(step, "b2", k, q))

    def pass_on(j):
        take("px", j)
        start("pf", j)

    def outer(j):
        if j == 0:
            for name in ("inner", "anchor", "momentum"):
                loads[name].wait()
        take("pm", j)
        take("pf", j)
        rows = slice(16 * j, 16 * j + 16)

        @pl.loop(0, D // 512)
        def _(i):
            cols = pl.ds(pl.multiple_of(i * 512, 512), 512)
            a = an[rows, cols]
            total = jnp.zeros_like(a)
            for n in range(4):
                total = total + (a - pb[n, rows, cols].astype(f32)) * not_spare[n]
            average = total / 3.0
            fresh = nesterov_mu * mo[rows, cols] + average
            an[rows, cols] = average
            w[rows, cols] = (a - outer_rate * (average + nesterov_mu * fresh)).astype(bf16)

    outs = {}

    def ship(name, i, src, dst):
        outs[name] = pltpu.make_async_copy(src, dst, out_sem.at[i])
        outs[name].start()

    for j in range(5):
        event(4 * (j + 1) + 2.5, functools.partial(pass_on, j))
        event(4 * (j + 1) + 5.5, functools.partial(outer, j))

    event(25.6, functools.partial(ship, "average", 0, an, average_out))

    def choose():
        for name in ("first", "second"):
            loads[name].wait()
        for i in range(2):
            take("mh", i)

            @pl.loop(0, HALF // 512)
            def _(n):
                cols = pl.ds(pl.multiple_of(n * 512, 512), 512)
                high = pl.ds(pl.multiple_of(n * 512 + HALF, 512), 512)
                mine = jnp.where(core == 0, fm[i, :, cols].astype(f32), fm[i, :, high].astype(f32))
                sel[i, :, cols] = jnp.where(peer == mate, mh[i, :, cols].astype(f32), mine).astype(bf16)

            start("mx", i)

    def settle(i):
        take("mx", i)

        @pl.loop(0, HALF // 512)
        def _(n):
            cols = pl.ds(pl.multiple_of(n * 512, 512), 512)
            here = jnp.logical_or(peer == r, peer == mate)
            ca[i, :, cols] = jnp.where(here, sel[i, :, cols].astype(f32), rx[i, :, cols].astype(f32)).astype(bf16)

        start("mc", i)

    def adopt(i):
        take("mc", i)

        @pl.loop(0, HALF // 512)
        def _(n):
            for half in range(2):
                cols = pl.ds(pl.multiple_of(n * 512, 512), 512)
                dest = pl.ds(pl.multiple_of(n * 512 + half * HALF, 512), 512)
                new = jnp.where(core == half, ca[i, :, cols].astype(f32), cb[i, :, cols].astype(f32))
                fm[i, :, dest] = jnp.where(spare == r, new, fm[i, :, dest].astype(f32)).astype(bf16)

    event(4.0, choose)
    for i in range(2):
        event(34.2 + 10 * i, functools.partial(settle, i))
        event(37.2 + 10 * i, functools.partial(adopt, i))
        event(37.2 + 10 * i, functools.partial(ship, ("first", "second")[i], i + 1, fm.at[i], (first_out, second_out)[i]))

    def prepare():
        for lo, hi in PADS:
            x[lo:hi, :] = jnp.zeros((hi - lo, D), bf16)
        for nth, blocks in enumerate((12, 16, 8)):
            n = blocks * BR
            out = lax.broadcasted_iota(jnp.int32, (n, n), 0)
            src = lax.broadcasted_iota(jnp.int32, (n, n), 1)
            quarter = (src % BR) // 4
            goal = quarter * (blocks * 4) + (src // BR) * 4 + src % 4
            perm[nth, 0:n, 0:n] = jnp.where(out == goal, 1.0, 0.0).astype(bf16)

    def reorder_cot(c):
        if c == 0:
            loads["cot"].wait()
            loads["table"].wait()
        cols = slice(256 * c, 256 * c + 256)
        dy, dz, other, t, void = (table_ref[i : i + 1, cols] for i in range(5))
        yy = dy + y
        yy = jnp.where(yy >= NY, yy - NY, yy)
        zz = dz + z
        zz = jnp.where(zz >= NZ, zz - NZ, zz)
        hh = jnp.where(other == 1, 1 - xh, xh)
        token = ((hh * NZ + zz) * NY + yy) * 4 + t
        token = jnp.where(void == 1, -1, token)
        pick = lax.broadcasted_iota(jnp.int32, (TOK, 256), 0) == token
        cotp[:, cols] = jnp.dot(cot[...], jnp.where(pick, 1.0, 0.0).astype(bf16), preferred_element_type=f32)

    def arrange(which, first, count, base):
        buf, per = (ga, NZ) if which == "a" else (gb, NY)
        blocks = per * count
        n = blocks * BR
        nth = {12: 0, 16: 1, 8: 2}[blocks]

        for i in range(BC // 256):
            cols = slice(i * 256, i * 256 + 256)
            got = jnp.dot(
                perm[nth, 0:n, 0:n], buf[first * per * BR : first * per * BR + n, cols], preferred_element_type=f32
            ).astype(bf16)
            for q in range(4):
                x[base : base + blocks * 4, q * BC + i * 256 : q * BC + i * 256 + 256] = got[
                    q * blocks * 4 : (q + 1) * blocks * 4
                ]

    def slopes(c):
        rows = slice(256 * c, 256 * c + 256)
        pre = lax.dot_general(w[...], x[rows, :], (((1,), (1,)), ((), ())), preferred_element_type=f32) / 64.0
        sigma = jax.nn.sigmoid(pre)
        gp[...] = (cotp[:, rows] * (sigma * (1.0 + pre * (1.0 - sigma)))).astype(bf16)

    def gradient(c):
        rows = slice(256 * c, 256 * c + 256)
        slopes(c)

        @pl.loop(0, D // 512)
        def _(i):
            cols = pl.ds(pl.multiple_of(i * 512, 512), 512)
            part = jnp.dot(gp[...], x[rows, cols], preferred_element_type=f32)
            if c == 0:
                acc[:, cols] = part
            else:
                acc[:, cols] += part

    event(0.5, prepare)
    for c in range(4):
        event(1.0 + 1.1 * c + (0.15 if c else 0), functools.partial(reorder_cot, c))
    for which, first, count, base in GROUPS:
        last = first + count - 1
        if last == 0:
            ready = 2.2 * 6 + 0.1 if which == "a" else 2.9 + 2.2 * 4 + 0.1
        else:
            hops = (last + 1) // 2
            ready = (a2_time if which == "a" else b2_time)(hops, 3) + 0.1
        event(ready, functools.partial(arrange, which, first, count, base))
    event(27.0, functools.partial(gradient, 0))
    event(38.3, functools.partial(gradient, 1))
    event(46.3, functools.partial(gradient, 2))

    for way in (1, -1):
        start("a1", way, 1)
    start("x")
    for j in range(5):
        start("px", j)
    for i in range(2):
        start("mh", i)
    for j in range(5):
        start("pm", j)
    for _, _, what in sorted(events, key=lambda e: e[:2]):
        what()

    slopes(3)
    for i in range(8):
        cols = slice(512 * i, 512 * i + 512)
        acc[:, cols] += jnp.dot(gp[...], x[768:1024, cols], preferred_element_type=f32)
        if i % 2:
            part = slice(512 * (i - 1), 512 * (i + 1))
            ship(("gradient", i // 2), 3 + i // 2, acc.at[:, part], gradient_out.at[:, part])

    assert received == set(made) and len(started) == len(made)
    for key in started:
        made[key].wait_send()
    for name in outs:
        outs[name].wait()


def local(inner_params, anchor, momentum, first_moment, second_moment, activations, cotangent, spare_index, peer_index):
    hbm = pl.BlockSpec(memory_space=pltpu.MemorySpace.HBM)
    dma = pltpu.SemaphoreType.DMA
    whole = jax.ShapeDtypeStruct((ROWS, D), f32)
    half = jax.ShapeDtypeStruct((ROWS, D), bf16)
    average, first_used, second_used, gradient = pl.pallas_call(
        kernel,
        out_shape=(whole, half, half, whole),
        in_specs=[hbm] * 10,
        out_specs=(hbm,) * 4,
        scratch_shapes=[
            pltpu.VMEM((NY * NZ * BR, BC), bf16),
            pltpu.VMEM((NY * NZ * BR, BC), bf16),
            pltpu.VMEM((1024, D), bf16),
            pltpu.VMEM((4, D), bf16),
            pltpu.VMEM((BR, BC), f32),
            pltpu.VMEM((4, ROWS, D), bf16),
            pltpu.VMEM((ROWS, D), f32),
            pltpu.VMEM((ROWS, D), f32),
            pltpu.VMEM((ROWS, D), bf16),
            pltpu.VMEM((2, ROWS, D), bf16),
            pltpu.VMEM((2, ROWS, HALF), bf16),
            pltpu.VMEM((2, ROWS, HALF), bf16),
            pltpu.VMEM((2, ROWS, HALF), bf16),
            pltpu.VMEM((2, ROWS, HALF), bf16),
            pltpu.VMEM((2, ROWS, HALF), bf16),
            pltpu.VMEM((ROWS, D), f32),
            pltpu.VMEM((ROWS, TOK), bf16),
            pltpu.VMEM((ROWS, 1024), f32),
            pltpu.VMEM((ROWS, 256), bf16),
            pltpu.VMEM((3, 256, 256), bf16),
            pltpu.VMEM((8, 1024), jnp.int32),
            pltpu.SMEM((1,), jnp.int32),
            pltpu.SMEM((1,), jnp.int32),
            dma((10,)),
            dma((NZ,)), dma((NZ,)),
            dma((NY, PIECES)), dma((NY, PIECES)),
            dma((NY,)), dma((NY,)),
            dma((NZ, PIECES)), dma((NZ, PIECES)),
            dma, dma,
            dma((3, 5)), dma((3, 5)),
            dma((3, 2)), dma((3, 2)),
            dma((7,)),
        ],
        compiler_params=pltpu.CompilerParams(
            collective_id=0, has_side_effects=True, vmem_limit_bytes=61 * 1024 * 1024
        ),
        cost_estimate=pl.CostEstimate(flops=2 * 2 * ROWS * D * TOK, bytes_accessed=9 << 20, transcendentals=ROWS * TOK),
    )(
        inner_params[0], anchor, momentum, first_moment[0], second_moment[0], activations[0], cotangent[0],
        spare_index, peer_index, jnp.asarray(token_table()),
    )
    momentum_new = nesterov_mu * momentum + average
    anchor_new = anchor - outer_rate * (average + nesterov_mu * momentum_new)
    gradient = gradient * (1.0 / 64.0)
    first = beta_one * first_used.astype(f32) + (1.0 - beta_one) * gradient
    second = beta_two * second_used.astype(f32) + (1.0 - beta_two) * gradient * gradient
    update = first / bias_one / (jnp.sqrt(second / bias_two) + adam_eps) + decay_rate * anchor_new
    return anchor_new, momentum_new, update[None]


def solution(mesh):
    placed = (
        P("replica", "shard", None),
        P("shard", None),
        P("shard", None),
        P("replica", "shard", None),
        P("replica", "shard", None),
        P("replica", "shard", None),
        P("replica", "shard", None),
        P("shard"),
        P("shard"),
    )
    return jax.shard_map(
        local,
        mesh=mesh,
        in_specs=placed,
        out_specs=(P("shard", None), P("shard", None), P("replica", "shard", None)),
        check_vma=False,
    )
```

```python
import functools

import jax
import jax.numpy as jnp
import numpy as np
from jax import lax
from jax.experimental import pallas as pl
from jax.experimental.pallas import tpu as pltpu
from jax.sharding import PartitionSpec as P

outer_rate = 0.7
nesterov_mu = 0.9
beta_one = 0.9
beta_two = 0.95
bias_one = 1.0 - 0.9**40
bias_two = 1.0 - 0.95**40
adam_eps = 1e-08
decay_rate = 0.1

NY, NZ = 8, 12
ROWS, D, TOK = 80, 4096, 768
HALF = D // 2
BR, BC = 16, 1024
PIECES = 4
ZP, YP = NZ // PIECES, NY // PIECES
f32, bf16 = jnp.float32, jnp.bfloat16


def slot(hops, way, ring):
    if hops == 0:
        return 0
    if 2 * hops == ring:
        return ring - 1
    return 2 * hops - 1 if way > 0 else 2 * hops


def offset_of(place, ring):
    if place == 0:
        return 0
    if place == ring - 1:
        return ring // 2
    hops = (place + 1) // 2
    return (ring - hops) if place % 2 else hops


GROUPS = [
    ("a", 0, 1, 0), ("a", 1, 1, 48), ("a", 2, 1, 96), ("b", 0, 1, 144), ("b", 1, 2, 176),
    ("a", 3, 1, 256), ("a", 4, 1, 304), ("b", 3, 2, 352), ("b", 5, 2, 416),
    ("a", 5, 1, 512), ("a", 6, 1, 560), ("b", 7, 2, 608),
    ("a", 7, 1, 768), ("b", 9, 2, 816), ("b", 11, 1, 880),
]
PADS = [(240, 256), (480, 512), (672, 768), (912, 1024)]


FROM_TWIN = [(0, 9), (0, 10), (0, 11), (1, 9), (1, 10), (1, 11), (2, 11), (3, 11)]


def token_table():
    table = np.zeros((8, 1024), np.int32)
    table[4] = 1
    for which, first, count, base in GROUPS:
        for row in range(first, first + count):
            for col in range(NZ if which == "a" else NY):
                yi, zi = (row, col) if which == "a" else (col, row)
                for t in range(4):
                    table[0, base] = offset_of(yi, NY)
                    table[1, base] = offset_of(zi, NZ)
                    table[2, base] = 0 if which == "a" else 1
                    table[3, base] = t
                    table[4, base] = 0
                    base += 1
    return table


def kernel(
    inner_ref, anchor_ref, momentum_ref, first_ref, second_ref, act_ref, cot_ref, spare_in, peer_in, table_in,
    average_out, first_out, second_out, gradient_out,
    ga, gb, x, act_v, act_f, pb, an, mo, w, fm, mh, sel, rx, ca, cb, acc, cot, cotp, gp, perm, table_ref, spare_ref, peer_ref,
    load_sem, a1_s, a1_r, a2_s, a2_r, b1_s, b1_r, b2_s, b2_r, x_s, x_r, xb_s, xb_r, p_s, p_r, m_s, m_r, out_sem,
):
    r = lax.axis_index("replica")
    s = lax.axis_index("shard")
    core = r % 2
    xlo = r // 2
    y = s % NY
    z = (s // NY) % NZ
    xh = s // (NY * NZ)
    mate = r + 1 - 2 * core
    across = (r + 2) % 4
    far_mate = mate + 2 - 4 * xlo

    def at(rep, sh):
        return {"replica": rep, "shard": sh}

    y_to = {1: at(r, s - y + (y + 1) % NY), -1: at(r, s - y + (y + NY - 1) % NY)}
    z_to = {
        1: at(r, (xh * NZ + (z + 1) % NZ) * NY + y),
        -1: at(r, (xh * NZ + (z + NZ - 1) % NZ) * NY + y),
    }
    plane_to = at(r, (s + NY * NZ) % (2 * NY * NZ))
    mate_to = at(mate, s)
    across_to = at(across, s)

    loads = {}

    def load(name, i, src, dst):
        loads[name] = pltpu.make_async_copy(src, dst, load_sem.at[i])
        loads[name].start()

    load("act", 0, act_ref, act_v)
    load("inner", 1, inner_ref, pb.at[0])
    load("anchor", 2, anchor_ref, an)
    load("momentum", 3, momentum_ref, mo)
    load("first", 4, first_ref, fm.at[0])
    load("second", 5, second_ref, fm.at[1])
    load("cot", 6, cot_ref, cot)
    load("table", 7, table_in, table_ref)
    load("spare", 8, spare_in, spare_ref)
    load("peer", 9, peer_in, peer_ref)

    barrier = pltpu.get_barrier_semaphore()
    for to in (y_to[1], y_to[-1], z_to[1], z_to[-1], plane_to, mate_to, across_to):
        pl.semaphore_signal(barrier, inc=1, device_id=to, device_id_type=pl.DeviceIdType.MESH)

    loads["act"].wait()
    for q in range(4):
        act_f[4 * q : 4 * q + 4, :] = act_v[:, q * BC : (q + 1) * BC].astype(f32)
    ga[0:BR, :] = act_f[...].astype(bf16)

    pl.semaphore_wait(barrier, 7)

    made = {}

    def copy(key, src, dst, ss, rs, to):
        made[key] = pltpu.make_async_remote_copy(
            src_ref=src, dst_ref=dst, send_sem=ss, recv_sem=rs, device_id=to, device_id_type=pl.DeviceIdType.MESH
        )

    def ga_at(yi, zi, n):
        return ga.at[pl.ds((yi * NZ + zi) * BR, n * BR), :]

    def gb_at(zi, yi, n):
        return gb.at[pl.ds((zi * NY + yi) * BR, n * BR), :]

    def has(hops, way, ring, piece=None):
        if 2 * hops < ring:
            return True
        if 2 * hops > ring:
            return False
        if piece is None:
            return way > 0
        return (way > 0) == (piece < PIECES // 2)

    def by_ring(k, way, q):
        if 2 * k < NZ:
            return (k, q) != (NZ // 2 - 1, 0)
        return q == (2 if way > 0 else 3)

    for i, (yi, zi) in enumerate(FROM_TWIN):
        copy(("xb", i), ga_at(yi, zi, 1), gb_at(zi, yi, 1), xb_s.at[i], xb_r.at[i], plane_to)
    for way in (1, -1):
        for k in range(1, NZ // 2 + 1):
            a, b = slot(k - 1, way, NZ), slot(k, way, NZ)
            if has(k, way, NZ):
                copy(("a1", way, k), ga_at(0, a, 1), ga_at(0, b, 1), a1_s.at[b], a1_r.at[b], z_to[way])
            for q in range(PIECES):
                if by_ring(k, way, q):
                    copy(("b2", way, k, q), gb_at(a, q * YP, YP), gb_at(b, q * YP, YP), b2_s.at[b, q], b2_r.at[b, q], z_to[way])
        for k in range(1, NY // 2 + 1):
            a, b = slot(k - 1, way, NY), slot(k, way, NY)
            if has(k, way, NY):
                copy(("b1", way, k), gb_at(0, a, 1), gb_at(0, b, 1), b1_s.at[b], b1_r.at[b], y_to[way])
            for q in range(PIECES):
                if has(k, way, NY, q):
                    copy(("a2", way, k, q), ga_at(a, q * ZP, ZP), ga_at(b, q * ZP, ZP), a2_s.at[b, q], a2_r.at[b, q], y_to[way])
    copy(("x",), ga_at(0, 0, 1), gb_at(0, 0, 1), x_s, x_r, plane_to)
    for j in range(5):
        rows = pl.ds(16 * j, 16)
        copy(("px", j), inner_ref.at[rows, :], pb.at[2, rows, :], p_s.at[0, j], p_r.at[0, j], across_to)
        copy(("pm", j), inner_ref.at[rows, :], pb.at[1, rows, :], p_s.at[1, j], p_r.at[1, j], mate_to)
        copy(("pf", j), pb.at[2, rows, :], pb.at[3, rows, :], p_s.at[2, j], p_r.at[2, j], mate_to)
    theirs = pl.ds(pl.multiple_of((1 - core) * HALF, HALF), HALF)
    for i, ref in enumerate((first_ref, second_ref)):
        copy(("mh", i), ref.at[:, theirs], mh.at[i], m_s.at[0, i], m_r.at[0, i], mate_to)
        copy(("mx", i), sel.at[i], rx.at[i], m_s.at[1, i], m_r.at[1, i], across_to)
        copy(("mc", i), ca.at[i], cb.at[i], m_s.at[2, i], m_r.at[2, i], mate_to)

    started, received, settled = [], set(), set()

    def clear():
        for key in started:
            if key in received and key not in settled:
                made[key].wait_send()
                settled.add(key)

    def start(*key):
        if key in made:
            made[key].start()
            assert key not in started
            started.append(key)

    def take(*key):
        if key in made:
            assert key in started and key not in received
            made[key].wait_recv()
            received.add(key)

    events = []

    def event(time, what):
        events.append((time, len(events), what))

    loads["spare"].wait()
    loads["peer"].wait()
    spare = spare_ref[0]
    peer = peer_ref[0]
    not_spare = [(spare != who).astype(f32) for who in (r, mate, across, far_mate)]

    def a1(k):
        for way in (1, -1):
            take("a1", way, k)
            start("a1", way, k + 1)

    def b1(k):
        for way in (1, -1):
            take("b1", way, k)
            start("b1", way, k + 1)

    def step(name, k, q):
        for way in (1, -1):
            if k:
                take(name, way, k, q)
            start(name, way, k + 1, q)

    def plane():
        take("x")
        start("b1", 1, 1)
        start("b1", -1, 1)

    a_in = {1: [0], 3: [1], 4: [2], 6: [3]}
    b_in = {1: [0], 2: [1], 3: [2], 4: [3]}
    for k in range(1, NZ // 2 + 1):
        event(2.2 * k, functools.partial(a1, k))
    event(2.9, plane)
    for k in range(1, NY // 2 + 1):
        event(2.9 + 2.2 * k, functools.partial(b1, k))
    for k, pieces in a_in.items():
        for q in pieces:
            event(2.2 * k + (0.8 if k == 1 else 0.01), functools.partial(step, "a2", 0, q))
    for k, pieces in b_in.items():
        for q in pieces:
            event(2.9 + 2.2 * k + 0.01, functools.partial(step, "b2", 0, q))

    def a2_time(k, q):
        return 6 + 12 * (k - 1) + 3 * ((q % 2 if 2 * k == NY else q) + 1) + 2

    def b2_time(k, q):
        return 10 + 8 * (k - 1) + 2 * ((q % 2 if 2 * k == NZ else q) + 1) + 2

    for q in range(PIECES):
        for k in range(1, NY // 2 + 1):
            event(a2_time(k, q), functools.partial(step, "a2", k, q))
        for k in range(1, NZ // 2 + 1):
            event(b2_time(k, q), functools.partial(step, "b2", k, q))

    def twin(act, *which):
        for i in which:
            act("xb", i)

    event(11.005, functools.partial(twin, start, 0, 1))
    event(13.205, functools.partial(twin, start, 2))
    event(20.001, functools.partial(twin, start, 3, 4, 5, 6))
    event(32.001, functools.partial(twin, start, 7))
    event(52.05, functools.partial(twin, take, 0, 1, 3, 4))
    event(56.05, functools.partial(twin, take, 2, 5, 6, 7))
    for time in (24.5, 36.5, 48.5, 53.6):
        event(time, clear)

    def pass_on(j):
        take("px", j)
        start("pf", j)

    def outer(j):
        if j == 0:
            for name in ("inner", "anchor", "momentum"):
                loads[name].wait()
        take("pm", j)
        take("pf", j)
        rows = slice(16 * j, 16 * j + 16)

        @pl.loop(0, D // 512)
        def _(i):
            cols = pl.ds(pl.multiple_of(i * 512, 512), 512)
            a = an[rows, cols]
            total = jnp.zeros_like(a)
            for n in range(4):
                total = total + (a - pb[n, rows, cols].astype(f32)) * not_spare[n]
            average = total / 3.0
            fresh = nesterov_mu * mo[rows, cols] + average
            an[rows, cols] = average
            w[rows, cols] = (a - outer_rate * (average + nesterov_mu * fresh)).astype(bf16)

    outs = {}

    def ship(name, i, src, dst):
        outs[name] = pltpu.make_async_copy(src, dst, out_sem.at[i])
        outs[name].start()

    for j in range(5):
        event(4 * (j + 1) + 2.5, functools.partial(pass_on, j))
        event(4 * (j + 1) + 5.5, functools.partial(outer, j))

    event(25.6, functools.partial(ship, "average", 0, an, average_out))

    def choose():
        for name in ("first", "second"):
            loads[name].wait()
        for i in range(2):
            take("mh", i)

            @pl.loop(0, HALF // 512)
            def _(n):
                cols = pl.ds(pl.multiple_of(n * 512, 512), 512)
                high = pl.ds(pl.multiple_of(n * 512 + HALF, 512), 512)
                mine = jnp.where(core == 0, fm[i, :, cols].astype(f32), fm[i, :, high].astype(f32))
                sel[i, :, cols] = jnp.where(peer == mate, mh[i, :, cols].astype(f32), mine).astype(bf16)

            start("mx", i)

    def settle(i):
        take("mx", i)

        @pl.loop(0, HALF // 512)
        def _(n):
            cols = pl.ds(pl.multiple_of(n * 512, 512), 512)
            here = jnp.logical_or(peer == r, peer == mate)
            ca[i, :, cols] = jnp.where(here, sel[i, :, cols].astype(f32), rx[i, :, cols].astype(f32)).astype(bf16)

        start("mc", i)

    def adopt(i):
        take("mc", i)

        @pl.loop(0, HALF // 512)
        def _(n):
            for half in range(2):
                cols = pl.ds(pl.multiple_of(n * 512, 512), 512)
                dest = pl.ds(pl.multiple_of(n * 512 + half * HALF, 512), 512)
                new = jnp.where(core == half, ca[i, :, cols].astype(f32), cb[i, :, cols].astype(f32))
                fm[i, :, dest] = jnp.where(spare == r, new, fm[i, :, dest].astype(f32)).astype(bf16)

    event(4.0, choose)
    for i in range(2):
        event(36.2 + 14 * i, functools.partial(settle, i))
        event(39.2 + 14 * i, functools.partial(adopt, i))
        event(39.2 + 14 * i, functools.partial(ship, ("first", "second")[i], i + 1, fm.at[i], (first_out, second_out)[i]))

    def prepare():
        for lo, hi in PADS:
            x[lo:hi, :] = jnp.zeros((hi - lo, D), bf16)
        for nth, blocks in enumerate((12, 16, 8)):
            n = blocks * BR
            out = lax.broadcasted_iota(jnp.int32, (n, n), 0)
            src = lax.broadcasted_iota(jnp.int32, (n, n), 1)
            quarter = (src % BR) // 4
            goal = quarter * (blocks * 4) + (src // BR) * 4 + src % 4
            perm[nth, 0:n, 0:n] = jnp.where(out == goal, 1.0, 0.0).astype(bf16)

    def reorder_cot(c):
        if c == 0:
            loads["cot"].wait()
            loads["table"].wait()
        cols = slice(256 * c, 256 * c + 256)
        dy, dz, other, t, void = (table_ref[i : i + 1, cols] for i in range(5))
        yy = dy + y
        yy = jnp.where(yy >= NY, yy - NY, yy)
        zz = dz + z
        zz = jnp.where(zz >= NZ, zz - NZ, zz)
        hh = jnp.where(other == 1, 1 - xh, xh)
        token = ((hh * NZ + zz) * NY + yy) * 4 + t
        token = jnp.where(void == 1, -1, token)
        pick = lax.broadcasted_iota(jnp.int32, (TOK, 256), 0) == token
        cotp[:, cols] = jnp.dot(cot[...], jnp.where(pick, 1.0, 0.0).astype(bf16), preferred_element_type=f32)

    def arrange(which, first, count, base):
        buf, per = (ga, NZ) if which == "a" else (gb, NY)
        blocks = per * count
        n = blocks * BR
        nth = {12: 0, 16: 1, 8: 2}[blocks]

        for i in range(BC // 256):
            cols = slice(i * 256, i * 256 + 256)
            got = jnp.dot(
                perm[nth, 0:n, 0:n], buf[first * per * BR : first * per * BR + n, cols], preferred_element_type=f32
            ).astype(bf16)
            for q in range(4):
                x[base : base + blocks * 4, q * BC + i * 256 : q * BC + i * 256 + 256] = got[
                    q * blocks * 4 : (q + 1) * blocks * 4
                ]

    def slopes(c):
        rows = slice(256 * c, 256 * c + 256)
        pre = lax.dot_general(w[...], x[rows, :], (((1,), (1,)), ((), ())), preferred_element_type=f32) / 64.0
        sigma = jax.nn.sigmoid(pre)
        gp[...] = (cotp[:, rows] * (sigma * (1.0 + pre * (1.0 - sigma)))).astype(bf16)

    def gradient(c):
        rows = slice(256 * c, 256 * c + 256)
        slopes(c)

        @pl.loop(0, D // 512)
        def _(i):
            cols = pl.ds(pl.multiple_of(i * 512, 512), 512)
            part = jnp.dot(gp[...], x[rows, cols], preferred_element_type=f32)
            if c == 0:
                acc[:, cols] = part
            else:
                acc[:, cols] += part

    event(0.5, prepare)
    for c in range(4):
        event(1.0 + 1.1 * c + (0.15 if c else 0), functools.partial(reorder_cot, c))
    for which, first, count, base in GROUPS:
        last = first + count - 1
        if last == 0:
            ready = 2.2 * 6 + 0.1 if which == "a" else 2.9 + 2.2 * 4 + 0.1
        else:
            hops = (last + 1) // 2
            ready = (a2_time if which == "a" else b2_time)(hops, 3) + 0.1
        event(ready, functools.partial(arrange, which, first, count, base))
    event(27.0, functools.partial(gradient, 0))
    event(38.3, functools.partial(gradient, 1))
    event(46.3, functools.partial(gradient, 2))

    for way in (1, -1):
        start("a1", way, 1)
    start("x")
    for j in range(5):
        start("px", j)
    for i in range(2):
        start("mh", i)
    for j in range(5):
        start("pm", j)
    for _, _, what in sorted(events, key=lambda e: e[:2]):
        what()

    slopes(3)
    for i in range(8):
        cols = slice(512 * i, 512 * i + 512)
        acc[:, cols] += jnp.dot(gp[...], x[768:1024, cols], preferred_element_type=f32)
        if i % 2:
            part = slice(512 * (i - 1), 512 * (i + 1))
            ship(("gradient", i // 2), 3 + i // 2, acc.at[:, part], gradient_out.at[:, part])

    assert received == set(made) and len(started) == len(made)
    clear()
    assert len(settled) == len(made)
    for name in outs:
        outs[name].wait()


def local(inner_params, anchor, momentum, first_moment, second_moment, activations, cotangent, spare_index, peer_index):
    hbm = pl.BlockSpec(memory_space=pltpu.MemorySpace.HBM)
    dma = pltpu.SemaphoreType.DMA
    whole = jax.ShapeDtypeStruct((ROWS, D), f32)
    half = jax.ShapeDtypeStruct((ROWS, D), bf16)
    average, first_used, second_used, gradient = pl.pallas_call(
        kernel,
        out_shape=(whole, half, half, whole),
        in_specs=[hbm] * 10,
        out_specs=(hbm,) * 4,
        scratch_shapes=[
            pltpu.VMEM((NY * NZ * BR, BC), bf16),
            pltpu.VMEM((NY * NZ * BR, BC), bf16),
            pltpu.VMEM((1024, D), bf16),
            pltpu.VMEM((4, D), bf16),
            pltpu.VMEM((BR, BC), f32),
            pltpu.VMEM((4, ROWS, D), bf16),
            pltpu.VMEM((ROWS, D), f32),
            pltpu.VMEM((ROWS, D), f32),
            pltpu.VMEM((ROWS, D), bf16),
            pltpu.VMEM((2, ROWS, D), bf16),
            pltpu.VMEM((2, ROWS, HALF), bf16),
            pltpu.VMEM((2, ROWS, HALF), bf16),
            pltpu.VMEM((2, ROWS, HALF), bf16),
            pltpu.VMEM((2, ROWS, HALF), bf16),
            pltpu.VMEM((2, ROWS, HALF), bf16),
            pltpu.VMEM((ROWS, D), f32),
            pltpu.VMEM((ROWS, TOK), bf16),
            pltpu.VMEM((ROWS, 1024), f32),
            pltpu.VMEM((ROWS, 256), bf16),
            pltpu.VMEM((3, 256, 256), bf16),
            pltpu.VMEM((8, 1024), jnp.int32),
            pltpu.SMEM((1,), jnp.int32),
            pltpu.SMEM((1,), jnp.int32),
            dma((10,)),
            dma((NZ,)), dma((NZ,)),
            dma((NY, PIECES)), dma((NY, PIECES)),
            dma((NY,)), dma((NY,)),
            dma((NZ, PIECES)), dma((NZ, PIECES)),
            dma, dma,
            dma((8,)), dma((8,)),
            dma((3, 5)), dma((3, 5)),
            dma((3, 2)), dma((3, 2)),
            dma((7,)),
        ],
        compiler_params=pltpu.CompilerParams(
            collective_id=0, has_side_effects=True, vmem_limit_bytes=61 * 1024 * 1024
        ),
        cost_estimate=pl.CostEstimate(flops=2 * 2 * ROWS * D * TOK, bytes_accessed=9 << 20, transcendentals=ROWS * TOK),
    )(
        inner_params[0], anchor, momentum, first_moment[0], second_moment[0], activations[0], cotangent[0],
        spare_index, peer_index, jnp.asarray(token_table()),
    )
    momentum_new = nesterov_mu * momentum + average
    anchor_new = anchor - outer_rate * (average + nesterov_mu * momentum_new)
    gradient = gradient * (1.0 / 64.0)
    first = beta_one * first_used.astype(f32) + (1.0 - beta_one) * gradient
    second = beta_two * second_used.astype(f32) + (1.0 - beta_two) * gradient * gradient
    update = first * (1.0 / bias_one) / (jnp.sqrt(second * (1.0 / bias_two)) + adam_eps) + decay_rate * anchor_new
    return anchor_new, momentum_new, update[None]


def solution(mesh):
    placed = (
        P("replica", "shard", None),
        P("shard", None),
        P("shard", None),
        P("replica", "shard", None),
        P("replica", "shard", None),
        P("replica", "shard", None),
        P("replica", "shard", None),
        P("shard"),
        P("shard"),
    )
    return jax.shard_map(
        local,
        mesh=mesh,
        in_specs=placed,
        out_specs=(P("shard", None), P("shard", None), P("replica", "shard", None)),
        check_vma=False,
    )
```
